128 devices in a mesh: in: 8 (over z, core), out: 16 (over x, y).
Axes of the slice: x: 4, y: 4, z: 4, core: 2. Of those that a mesh axis runs over, the one named last changes fastest.
Arguments:
- activations: bfloat16 [1024, 5120], P('out', 'in'), may hold values from -6 to 6
- act_basis: bfloat16 [5120, 5120], P(None, 'in'), may hold values from -0.078125 to 0.078125
- gradients: bfloat16 [1024, 20480], P('out', 'in'), may hold values from -0.59765625 to 0.59765625
- grad_basis: bfloat16 [20480, 20480], P('in', 'out'), may hold values from -0.0390625 to 0.0390625
- lengths: int32 [8], replicated, may hold values from 1 to 128, 768 in all
- sample_weights: int32 [8], replicated, may hold values from 1 to 4
Outputs:
- eigenvalues: float32 [20480, 5120], P('out', 'in')
The draws below stay inside these ranges and needn't reach their ends.
Inputs may be any that keep to these rules, and one draw needn't show every extreme that they name: Some sequence is full, every sequence has at least one valid token, and the lengths sum to 768.
All inputs are finite; a program needn't handle non-finite values.
Results may differ from the reference program's by a relative error of at most 0.0031.
Values may be sent and summed in bfloat16 or wider, within the bound.
A program may use at most 128 MiB of HBM per device.

```python
import math
import jax
import jax.numpy as jnp
import numpy as np
from jax import lax

DIN = 5120
DOUT = 20480
LEN = 128
SEQS = 8
TOKENS = 1024


def set_ends(array, rng, least, largest):
    spot = [jax.random.randint(jax.random.fold_in(rng, axis), (), 0, length) for axis, length in enumerate(array.shape)]
    main_axis = array.shape.index(max(array.shape))
    next_to = spot[:main_axis] + [(spot[main_axis] + 1) % array.shape[main_axis]] + spot[main_axis + 1:]
    return array.at[tuple(spot)].set(least).at[tuple(next_to)].set(largest)


def levels(own_key, dims, shards, low, largest):
    loudness, own = 1.0, jax.random.fold_in(own_key, 6)
    for axis_at, blocks in shards:
        steps = jnp.exp(jax.random.uniform(jax.random.fold_in(own, axis_at), (blocks,), jnp.float32, low / len(shards), largest / len(shards)))
        loudness = loudness * jnp.repeat(steps, dims[axis_at] // blocks).reshape([-1 if axis == axis_at else 1 for axis in range(len(dims))])
    return loudness


def length_profile(amount, total, bound, slope):
    loads = [(1 << 20) // math.isqrt(rank ** slope) + 1 for rank in range(2, amount + 1)]
    rest, holding = total - bound - (amount - 1), [1] * (amount - 1)
    while rest > 0:
        free = [i for i in range(amount - 1) if holding[i] < bound]
        pool, remaining = sum([loads[i] for i in free]), rest
        for i in free:
            more = min(bound - holding[i], max(1, remaining * loads[i] // pool), rest)
            holding[i] = holding[i] + more
            rest = rest - more
    return np.array([bound] + holding)


def ragged(key, number_of, total, limit, slope):
    if number_of == 2:
        one = jax.random.randint(key, (), max(1, total - limit), min(limit, total - 1) + 1)
        return jnp.stack([one, total - one])
    tallies = jnp.asarray(length_profile(number_of, total, limit, slope), jnp.int32)
    pairs = (number_of - 1) // 2
    giver, sink = tallies[1:1 + 2 * pairs:2], tallies[2:2 + 2 * pairs:2]
    margin = jnp.minimum(giver - 1, limit - sink)
    moved = jax.random.randint(jax.random.fold_in(key, 1), (pairs,), 0, 1 << 20) % (margin + 1)
    tallies = tallies.at[1:1 + 2 * pairs:2].set(giver - moved).at[2:2 + 2 * pairs:2].set(sink + moved)
    return tallies[jax.random.permutation(jax.random.fold_in(key, 2), number_of)]


def bell_draw(rng, shape, width, limit, split=(), kind=jnp.bfloat16):
    result = jax.random.normal(rng, shape, jnp.float32) * width
    if len(split) > 0:
        result = levels(rng, shape, split, -0.22, 0.18) * result
    return jnp.clip(result, min=-limit, max=limit).astype(kind)


def setup_inputs(seed: int = 0) -> dict:
    key_of = jax.random.split(jax.random.key(seed), 7)
    activations = bell_draw(key_of[0], (TOKENS, DIN), 1.0, 6.0, ((0, 16), (1, 8)))
    act_basis = bell_draw(key_of[1], (DIN, DIN), DIN ** -0.5, 0.078125, ((1, 8),))
    gradients = bell_draw(key_of[2], (TOKENS, DOUT), 0.09, 0.59765625, ((0, 16), (1, 8)))
    grad_basis = bell_draw(key_of[3], (DOUT, DOUT), DOUT ** -0.5, 0.0390625, ((0, 8), (1, 16)))
    lengths = ragged(key_of[4], SEQS, SEQS * LEN * 3 // 4, LEN, 2).astype(jnp.int32)
    sample_weights = set_ends(jax.random.randint(key_of[5], (SEQS,), 1, 5), jax.random.fold_in(key_of[5], 1), 1, 4).astype(jnp.int32)
    return {"activations": activations, "act_basis": act_basis, "gradients": gradients, "grad_basis": grad_basis, "lengths": lengths, "sample_weights": sample_weights}


def reference(activations, act_basis, gradients, grad_basis, lengths, sample_weights):
    rot_act = jnp.dot(activations, act_basis, preferred_element_type=jnp.float32).astype(jnp.bfloat16)
    rot_grad = jnp.dot(gradients, grad_basis, preferred_element_type=jnp.float32).astype(jnp.bfloat16)
    positions = jnp.arange(LEN, dtype=jnp.int32)
    valid = (positions[None, :] < lengths[:, None]).astype(rot_grad.dtype)
    act_seq = rot_act.reshape(SEQS, LEN, DIN)
    grad_seq = rot_grad.reshape(SEQS, LEN, DOUT) * valid[:, :, None]
    weights = sample_weights.astype(jnp.float32)

    def accumulate(total, item):
        grad_one, act_one, weight = item
        block = lax.dot_general(grad_one, act_one, (((0,), (0,)), ((), ())), preferred_element_type=jnp.float32)
        return total + weight * block * block, None

    start = jnp.zeros((DOUT, DIN), jnp.float32)
    total, unused = lax.scan(accumulate, start, (grad_seq, act_seq, weights))
    return total / jnp.sum(weights)
```

```python
import functools

import jax
import jax.numpy as jnp
from jax import lax
from jax.experimental import pallas as pl
from jax.experimental.pallas import tpu as pltpu
from jax.sharding import PartitionSpec as P

MESH = pl.DeviceIdType.MESH
HALF = 32
STAGES = ("own", "1", "2", "3a", "3b", "4b", "5b", "6", "7a", "7b", "8")
BRINGS = {
    "own": [(0, 0)],
    "1": [(1, 0), (-1, 0)],
    "2": [(0, 1), (0, -1)],
    "3a": [(2, 0)],
    "3b": [(1, 1), (1, -1)],
    "4b": [(-1, 1), (-1, -1)],
    "5b": [(0, 2)],
    "6": [(2, 1), (2, -1)],
    "7a": [(1, 2)],
    "7b": [(-1, 2)],
    "8": [(2, 2)],
}
SLOTS = [(lane, a, b) for stage in STAGES for lane in (0, 1) for a, b in BRINGS[stage]]
OFFSET = {slot: HALF * at for at, slot in enumerate(SLOTS)}
GROUPS = [(0, 192), (192, 128), (320, 192), (512, 192), (704, 128), (832, 128), (960, 64)]


def moves(stage):
    found = []
    for lane in (0, 1):
        for sign in (1, -1):
            part = 1 if sign == 1 else 2
            one = {
                "1": ((0, 0), (-sign, 0), 0, 0),
                "2": ((0, 0), (0, -sign), 1, 0),
                "3a": ((-sign, 0), (2, 0), 0, part),
                "3b": ((1, 0), (1, -sign), 1, 0),
                "4b": ((-1, 0), (-1, -sign), 1, 0),
                "5b": ((0, -sign), (0, 2), 1, part),
                "6": ((2, 0), (2, -sign), 1, 0),
                "7a": ((1, -sign), (1, 2), 1, part),
                "7b": ((-1, -sign), (-1, 2), 1, part),
                "8": ((2, -sign), (2, 2), 1, part),
            }[stage]
            found.append((lane, one[0], one[1], one[2], sign, one[3]))
    return found


def rows_of(part):
    return (0, HALF) if part == 0 else ((0, HALF // 2) if part == 1 else (HALF // 2, HALF // 2))


def kernel(
    act_ref, w_ref, g_ref, u_ref, len_ref, wt_ref, out_ref,
    u, w, gb, pf, cs, cr, sb, rr, rb, rabs, ra, ab, acc,
    load_sem, xy_send, xy_recv, core_send, core_recv, rs_send, rs_recv,
    ag_send, ag_recv, fw_send, fw_recv, co_send, co_recv, az_send, az_recv, ac_send, ac_recv, out_sem,
):
    i, o = lax.axis_index("in"), lax.axis_index("out")
    z, c = lax.div(i, 2), lax.rem(i, 2)
    x, y = lax.div(o, 4), lax.rem(o, 4)
    width = ra.shape[1]
    half = rb.shape[2]

    def xy(axis, sign):
        if axis == 0:
            return (i, lax.rem(x + sign + 4, 4) * 4 + y)
        return (i, x * 4 + lax.rem(y + sign + 4, 4))

    def chip(d):
        return (lax.rem(z + d, 4) * 2 + c, o)

    other = (z * 2 + 1 - c, o)
    pending = []

    g_load = pltpu.make_async_copy(g_ref, gb.at[pl.ds(0, 2 * HALF)], load_sem.at[0])
    mine = pl.ds(pl.multiple_of(i * width, 128), width)
    a_load = pltpu.make_async_copy(act_ref, ab.at[:, mine], load_sem.at[1])
    u_load = pltpu.make_async_copy(u_ref, u, load_sem.at[2])
    w_load = pltpu.make_async_copy(w_ref, w, load_sem.at[3])
    for load in (g_load, a_load, u_load, w_load):
        load.start()

    peers = [xy(0, 1), xy(0, -1), xy(1, 1), xy(1, -1), chip(1), chip(2), chip(3), other]
    barrier = pltpu.get_barrier_semaphore()
    for peer in peers:
        pl.semaphore_signal(barrier, inc=1, device_id=peer, device_id_type=MESH)
    pl.semaphore_wait(barrier, len(peers))

    def remote(src, dst, send, recv, device):
        return pltpu.make_async_remote_copy(
            src_ref=src, dst_ref=dst, send_sem=send, recv_sem=recv, device_id=device, device_id_type=MESH
        )

    def token(lane, a, b):
        dx, dy = (b, a) if lane == 0 else (a, b)
        shard = lax.rem(x + dx + 4, 4) * 4 + lax.rem(y + dy + 4, 4)
        return shard * 2 * HALF + lane * HALF

    def xy_copy(kind, stage, at, arriving):
        lane, src, dst, axis, sign, part = moves(stage)[at]
        number = 4 * STAGES.index(stage) - 4 + at
        start, size = rows_of(part)
        if kind == 0:
            from_row, to_row, ref = OFFSET[(lane, *src)] + start, OFFSET[(lane, *dst)] + start, gb
        else:
            ref = ra
            from_row = pl.multiple_of(token(lane, *src) + start, 16)
            to_row = pl.multiple_of(token(lane, *dst) + start, 16) if arriving else from_row
        return remote(
            ref.at[pl.ds(from_row, size)], ref.at[pl.ds(to_row, size)],
            xy_send.at[kind, number], xy_recv.at[kind, number],
            xy(1 - axis if lane == 0 else axis, sign),
        )

    def issue(kind, *stages):
        for stage in stages:
            for at in range(4):
                copy = xy_copy(kind, stage, at, False)
                copy.start()
                pending.append(copy)

    def arrive(kind, *stages):
        for stage in stages:
            for at in range(4):
                xy_copy(kind, stage, at, True).wait_recv()

    own_cols = pl.ds(pl.multiple_of(c * half, 128), half)
    other_cols = pl.ds(pl.multiple_of((1 - c) * half, 128), half)

    def core_copy(q):
        row, m = GROUPS[q]
        return remote(cs.at[pl.ds(row, m)], cr.at[pl.ds(row, m)], core_send.at[q], core_recv.at[q], other)

    def s1(q):
        row, m = GROUPS[q]

        def tile(n, carry):
            cols = pl.ds(pl.multiple_of(n * 256, 256), 256)
            pf[pl.ds(row, m), cols] = jnp.dot(gb[pl.ds(row, m)], u[:, cols], preferred_element_type=jnp.float32)
            return carry

        lax.fori_loop(0, pf.shape[1] // 256, tile, 0)
        cs[pl.ds(row, m)] = pf[pl.ds(row, m), other_cols].astype(cs.dtype)
        copy = core_copy(q)
        copy.start()
        pending.append(copy)

    def rs_copy(q, d):
        row, m = GROUPS[q]
        n = m // 4
        there = lax.rem(z + d, 4)
        return remote(
            sb.at[pl.ds(pl.multiple_of(row + there * n, 16), n)], rr.at[d - 1, pl.ds(row // 4, n)],
            rs_send.at[q, d - 1], rs_recv.at[q, d - 1], chip(d),
        )

    def s2(q):
        row, m = GROUPS[q]
        core_copy(q).wait_recv()
        sb[pl.ds(row, m)] = (pf[pl.ds(row, m), own_cols] + cr[pl.ds(row, m)].astype(jnp.float32)).astype(sb.dtype)
        for d in (2, 1, 3):
            copy = rs_copy(q, d)
            copy.start()
            pending.append(copy)

    def piece(q, there):
        row, m = GROUPS[q]
        return pl.multiple_of(row + there * (m // 4), 16)

    def ag_copy(q, d, arriving):
        n = GROUPS[q][1] // 4
        at = piece(q, lax.rem(z - d + 4, 4) if arriving else z)
        block = rb.at[c, pl.ds(at, n)]
        return remote(block, block, ag_send.at[q, d - 1], ag_recv.at[q, d - 1], chip(d))

    def far(q):
        return GROUPS[q][1] < 128

    def s3(q):
        row, m = GROUPS[q]
        n = m // 4
        for d in (1, 2, 3):
            rs_copy(q, d).wait_recv()
        at = pl.ds(piece(q, z), n)
        total = pf[at, own_cols] + cr[at].astype(jnp.float32)
        for d in (1, 2, 3):
            total = total + rr[d - 1, pl.ds(row // 4, n)].astype(jnp.float32)
        rb[c, at] = total.astype(rb.dtype)
        for d in (2, 1, 3) if far(q) else (1, 3):
            copy = ag_copy(q, d, False)
            copy.start()
            pending.append(copy)

    def fw_copy(q, way, arriving):
        n = GROUPS[q][1] // 4
        first = n // 32 * 16
        start, size = (0, first) if way == 0 else (first, n - first)
        at = piece(q, lax.rem(z + 2, 4) if arriving else lax.rem(z + (3 if way == 0 else 1), 4)) + start
        block = rb.at[c, pl.ds(pl.multiple_of(at, 16), size)]
        return remote(block, block, fw_send.at[q, way], fw_recv.at[q, way], chip(1 if way == 0 else 3))

    def s3b(q):
        if far(q):
            return
        for d, way in ((1, 0), (3, 1)):
            ag_copy(q, d, True).wait_recv()
            copy = fw_copy(q, way, False)
            copy.start()
            pending.append(copy)

    def co_copy(q, arriving):
        row, m = GROUPS[q]
        block = rb.at[1 - c if arriving else c, pl.ds(row, m)]
        return remote(block, block, co_send.at[q], co_recv.at[q], other)

    def s4(q):
        if far(q):
            for d in (1, 2, 3):
                ag_copy(q, d, True).wait_recv()
        else:
            for way in (0, 1):
                fw_copy(q, way, True).wait_recv()
        copy = co_copy(q, False)
        copy.start()
        pending.append(copy)

    def s5(q):
        row, m = GROUPS[q]
        co_copy(q, True).wait_recv()
        for at in range(row // HALF, (row + m) // HALF):
            first = pl.multiple_of(token(*SLOTS[at]), 16)
            length = len_ref[lax.div(first, 4 * HALF)]
            position = lax.broadcasted_iota(jnp.int32, (HALF, half), 0) + lax.rem(first, 4 * HALF)
            for h in (0, 1):
                block = rb[h, pl.ds(at * HALF, HALF)].astype(jnp.float32)
                rabs[pl.ds(first, HALF), pl.ds(h * half, half)] = jnp.where(position < length, block, 0.0).astype(rabs.dtype)

    def az_copy(d, arriving):
        from_z = lax.rem(z - d + 4, 4) if arriving else z
        block = ab.at[:, pl.ds(pl.multiple_of((from_z * 2 + c) * width, 128), width)]
        return remote(block, block, az_send.at[d - 1], az_recv.at[d - 1], chip(d))

    def ac_copy(d, arriving):
        there = lax.rem(z + d, 4) * 2 + (1 - c if arriving else c)
        block = ab.at[:, pl.ds(pl.multiple_of(there * width, 128), width)]
        return remote(block, block, ac_send.at[d], ac_recv.at[d], other)

    def rotate_act():
        for d in range(4):
            ac_copy(d, True).wait_recv()
        w_load.wait()
        first = pl.multiple_of(o * 2 * HALF, 16)
        for start in range(0, width, 256):
            size = min(256, width - start)
            ra[pl.ds(first, 2 * HALF), pl.ds(start, size)] = jnp.dot(
                ab[...], w[:, pl.ds(start, size)], preferred_element_type=jnp.float32
            ).astype(ra.dtype)

    h0 = lax.div(y, 2)
    sequences = [
        x * 2 + h0, x * 2 + 1 - h0,
        lax.rem(x + 1, 4) * 2 + h0, lax.rem(x + 3, 4) * 2 + h0,
        lax.rem(x + 1, 4) * 2 + 1 - h0, lax.rem(x + 3, 4) * 2 + 1 - h0,
        lax.rem(x + 2, 4) * 2 + h0, lax.rem(x + 2, 4) * 2 + 1 - h0,
    ]
    weight_sum = wt_ref[0]
    for n in range(1, 8):
        weight_sum = weight_sum + wt_ref[n]
    weight_sum = weight_sum.astype(jnp.float32)
    tile_rows = 256

    def out_copy(j):
        rows = pl.ds(pl.multiple_of(j * tile_rows, 8), tile_rows)
        return pltpu.make_async_copy(acc.at[rows], out_ref.at[rows], out_sem.at[j])

    def final(batch, last):
        def tile(j, carry):
            cols = pl.ds(pl.multiple_of(j * tile_rows, tile_rows), tile_rows)
            total = None if batch[0] == 0 else acc[cols]
            for s in batch:
                rows = pl.ds(pl.multiple_of(sequences[s] * 128, 128), 128)
                block = lax.dot_general(
                    rabs[rows, cols], ra[rows], (((0,), (0,)), ((), ())), preferred_element_type=jnp.float32
                )
                term = wt_ref[sequences[s]].astype(jnp.float32) * block * block
                total = term if total is None else total + term
            if last:
                acc[cols] = total / weight_sum
                out_copy(j).start()
            else:
                acc[cols] = total
            return carry

        lax.fori_loop(0, acc.shape[0] // tile_rows, tile, 0)

    g_load.wait()
    issue(0, "1", "2")
    a_load.wait()
    for d in (2, 1, 3):
        copy = az_copy(d, False)
        copy.start()
        pending.append(copy)
    u_load.wait()

    arrive(0, "1")
    issue(0, "3a", "3b", "4b")
    s1(0)
    for d in (0, 1, 2, 3):
        if d:
            az_copy(4 - d, True).wait_recv()
        copy = ac_copy(d, False)
        copy.start()
        pending.append(copy)

    arrive(0, "2")
    issue(0, "5b")
    s2(0)
    s1(1)
    rotate_act()

    arrive(0, "3a")
    issue(0, "6")
    arrive(0, "3b")
    issue(0, "7a")
    s3(0)
    s2(1)
    s1(2)

    arrive(0, "4b")
    issue(0, "7b")
    arrive(0, "5b")
    s3b(0)
    s3(1)
    s2(2)
    s1(3)

    arrive(0, "6")
    issue(0, "8")
    issue(1, "1", "2")
    s4(0)
    s3b(1)
    s3(2)
    s2(3)
    s1(4)

    arrive(0, "7a", "7b")
    s5(0)
    s4(1)
    s3b(2)
    s3(3)
    s2(4)
    s1(5)

    arrive(0, "8")
    s1(6)
    s2(5)
    s3(4)
    s3b(3)
    s4(2)
    s5(1)

    s2(6)
    arrive(1, "1")
    issue(1, "3a", "3b", "4b")
    arrive(1, "2")
    issue(1, "5b")
    s3(5)
    s3b(4)
    s4(3)
    s5(2)

    s3(6)
    arrive(1, "3a")
    issue(1, "6")
    arrive(1, "3b")
    issue(1, "7a")
    s3b(5)
    s4(4)
    s5(3)

    arrive(1, "4b")
    issue(1, "7b")
    arrive(1, "5b")
    s4(5)
    s4(6)
    arrive(1, "6")
    issue(1, "8")
    final((0, 1, 2, 3), False)
    s5(4)
    s5(5)
    arrive(1, "7a", "7b")
    final((4, 5, 6), False)
    s5(6)
    arrive(1, "8")
    final((7,), True)

    for copy in pending:
        copy.wait_send()
    for j in range(acc.shape[0] // tile_rows):
        out_copy(j).wait()


def local(activations, act_basis, gradients, grad_basis, lengths, sample_weights):
    rows, wide = gradients.shape
    depth, cols = grad_basis.shape
    full, width = act_basis.shape
    tokens = 16 * rows
    groups = len(GROUPS)
    bf16, f32 = jnp.bfloat16, jnp.float32
    dma = pltpu.SemaphoreType.DMA
    anywhere = pl.BlockSpec(memory_space=pl.ANY)
    scalars = pl.BlockSpec(memory_space=pltpu.SMEM)
    return pl.pallas_call(
        kernel,
        out_shape=jax.ShapeDtypeStruct((cols, width), f32),
        in_specs=[anywhere] * 4 + [scalars] * 2,
        out_specs=anywhere,
        scratch_shapes=[
            pltpu.VMEM((depth, cols), bf16),
            pltpu.VMEM((full, width), bf16),
            pltpu.VMEM((tokens, wide), bf16),
            pltpu.VMEM((tokens, cols), f32),
            pltpu.VMEM((tokens, cols // 2), bf16),
            pltpu.VMEM((tokens, cols // 2), bf16),
            pltpu.VMEM((tokens, cols // 2), bf16),
            pltpu.VMEM((3, tokens // 4, cols // 2), bf16),
            pltpu.VMEM((2, tokens, cols // 2), bf16),
            pltpu.VMEM((tokens, cols), bf16),
            pltpu.VMEM((tokens, width), bf16),
            pltpu.VMEM((rows, full), bf16),
            pltpu.VMEM((cols, width), f32),
            dma((4,)),
            dma((2, 40)), dma((2, 40)),
            dma((groups,)), dma((groups,)),
            dma((groups, 3)), dma((groups, 3)),
            dma((groups, 3)), dma((groups, 3)),
            dma((groups, 2)), dma((groups, 2)),
            dma((groups,)), dma((groups,)),
            dma((3,)), dma((3,)),
            dma((4,)), dma((4,)),
            dma((cols // 256,)),
        ],
        compiler_params=pltpu.CompilerParams(
            collective_id=0, has_side_effects=True, vmem_limit_bytes=56 * 1024 * 1024
        ),
    )(activations, act_basis, gradients, grad_basis, lengths, sample_weights)


def solution(mesh):
    in_specs = (P("out", "in"), P(None, "in"), P("out", "in"), P("in", "out"), P(), P())
    return jax.shard_map(local, mesh=mesh, in_specs=in_specs, out_specs=P("out", "in"), check_vma=False)
```

```python
import functools

import jax
import jax.numpy as jnp
from jax import lax
from jax.experimental import pallas as pl
from jax.experimental.pallas import tpu as pltpu
from jax.sharding import PartitionSpec as P

MESH = pl.DeviceIdType.MESH
HALF = 32
STAGES = ("own", "1", "2", "3a", "3b", "4b", "5b", "6", "7a", "7b", "8")
BRINGS = {
    "own": [(0, 0)],
    "1": [(1, 0), (-1, 0)],
    "2": [(0, 1), (0, -1)],
    "3a": [(2, 0)],
    "3b": [(1, 1), (1, -1)],
    "4b": [(-1, 1), (-1, -1)],
    "5b": [(0, 2)],
    "6": [(2, 1), (2, -1)],
    "7a": [(1, 2)],
    "7b": [(-1, 2)],
    "8": [(2, 2)],
}
SLOTS = [(lane, a, b) for stage in STAGES for lane in (0, 1) for a, b in BRINGS[stage]]
OFFSET = {slot: HALF * at for at, slot in enumerate(SLOTS)}
GROUPS = [(0, 192), (192, 128), (320, 192), (512, 192), (704, 128), (832, 128), (960, 64)]


def moves(stage):
    found = []
    for lane in (0, 1):
        for sign in (1, -1):
            part = 1 if sign == 1 else 2
            one = {
                "1": ((0, 0), (-sign, 0), 0, 0),
                "2": ((0, 0), (0, -sign), 1, 0),
                "3a": ((-sign, 0), (2, 0), 0, part),
                "3b": ((1, 0), (1, -sign), 1, 0),
                "4b": ((-1, 0), (-1, -sign), 1, 0),
                "5b": ((0, -sign), (0, 2), 1, part),
                "6": ((2, 0), (2, -sign), 1, 0),
                "7a": ((1, -sign), (1, 2), 1, part),
                "7b": ((-1, -sign), (-1, 2), 1, part),
                "8": ((2, -sign), (2, 2), 1, part),
            }[stage]
            found.append((lane, one[0], one[1], one[2], sign, one[3]))
    return found


def rows_of(part):
    return (0, HALF) if part == 0 else ((0, HALF // 2) if part == 1 else (HALF // 2, HALF // 2))


def kernel(
    act_ref, w_ref, g_ref, u_ref, len_ref, wt_ref, out_ref,
    u, w, gb, pf, cs, cr, sb, rr, rb, rabs, ra, ab, acc,
    load_sem, xy_send, xy_recv, core_send, core_recv, rs_send, rs_recv,
    ag_send, ag_recv, fw_send, fw_recv, co_send, co_recv, az_send, az_recv, ac_send, ac_recv, out_sem,
):
    i, o = lax.axis_index("in"), lax.axis_index("out")
    z, c = lax.div(i, 2), lax.rem(i, 2)
    x, y = lax.div(o, 4), lax.rem(o, 4)
    width = ra.shape[1]
    half = rb.shape[2]

    def xy(axis, sign):
        if axis == 0:
            return (i, lax.rem(x + sign + 4, 4) * 4 + y)
        return (i, x * 4 + lax.rem(y + sign + 4, 4))

    def chip(d):
        return (lax.rem(z + d, 4) * 2 + c, o)

    other = (z * 2 + 1 - c, o)
    pending = []

    g_load = pltpu.make_async_copy(g_ref, gb.at[pl.ds(0, 2 * HALF)], load_sem.at[0])
    mine = pl.ds(pl.multiple_of(i * width, 128), width)
    a_load = pltpu.make_async_copy(act_ref, ab.at[:, mine], load_sem.at[1])
    u_load = pltpu.make_async_copy(u_ref, u, load_sem.at[2])
    w_load = pltpu.make_async_copy(w_ref, w, load_sem.at[3])
    for load in (g_load, a_load, u_load, w_load):
        load.start()

    peers = [xy(0, 1), xy(0, -1), xy(1, 1), xy(1, -1), chip(1), chip(2), chip(3), other]
    barrier = pltpu.get_barrier_semaphore()
    for peer in peers:
        pl.semaphore_signal(barrier, inc=1, device_id=peer, device_id_type=MESH)
    pl.semaphore_wait(barrier, len(peers))

    def remote(src, dst, send, recv, device):
        return pltpu.make_async_remote_copy(
            src_ref=src, dst_ref=dst, send_sem=send, recv_sem=recv, device_id=device, device_id_type=MESH
        )

    def token(lane, a, b):
        dx, dy = (b, a) if lane == 0 else (a, b)
        shard = lax.rem(x + dx + 4, 4) * 4 + lax.rem(y + dy + 4, 4)
        return shard * 2 * HALF + lane * HALF

    def xy_copy(kind, stage, at, arriving):
        lane, src, dst, axis, sign, part = moves(stage)[at]
        number = 4 * STAGES.index(stage) - 4 + at
        start, size = rows_of(part)
        if kind == 0:
            from_row, to_row, ref = OFFSET[(lane, *src)] + start, OFFSET[(lane, *dst)] + start, gb
        else:
            ref = ra
            from_row = pl.multiple_of(token(lane, *src) + start, 16)
            to_row = pl.multiple_of(token(lane, *dst) + start, 16) if arriving else from_row
        return remote(
            ref.at[pl.ds(from_row, size)], ref.at[pl.ds(to_row, size)],
            xy_send.at[kind, number], xy_recv.at[kind, number],
            xy(1 - axis if lane == 0 else axis, sign),
        )

    def issue(kind, *stages):
        for stage in stages:
            for at in range(4):
                copy = xy_copy(kind, stage, at, False)
                copy.start()
                pending.append(copy)

    def arrive(kind, *stages):
        for stage in stages:
            for at in range(4):
                xy_copy(kind, stage, at, True).wait_recv()

    def core_copy(q):
        row, m = GROUPS[q]
        return remote(cs.at[pl.ds(row, m)], cr.at[pl.ds(row, m)], core_send.at[q], core_recv.at[q], other)

    def s1(q):
        row, m = GROUPS[q]
        rows = pl.ds(row, m)

        def side(n, carry):
            cols = pl.ds(pl.multiple_of(lax.rem(1 - c + n, 2) * half, 128), half)
            pf[rows] = jnp.dot(gb[rows], u[:, cols], preferred_element_type=jnp.float32)

            @pl.when(n == 0)
            def _():
                cs[rows] = pf[rows].astype(cs.dtype)
                core_copy(q).start()

            return carry

        lax.fori_loop(0, 2, side, 0)
        pending.append(core_copy(q))

    def rs_copy(q, d):
        row, m = GROUPS[q]
        n = m // 4
        there = lax.rem(z + d, 4)
        return remote(
            sb.at[pl.ds(pl.multiple_of(row + there * n, 16), n)], rr.at[d - 1, pl.ds(row // 4, n)],
            rs_send.at[q, d - 1], rs_recv.at[q, d - 1], chip(d),
        )

    def s2(q):
        row, m = GROUPS[q]
        core_copy(q).wait_recv()
        sb[pl.ds(row, m)] = (pf[pl.ds(row, m)] + cr[pl.ds(row, m)].astype(jnp.float32)).astype(sb.dtype)
        for d in (2, 1, 3):
            copy = rs_copy(q, d)
            copy.start()
            pending.append(copy)

    def piece(q, there):
        row, m = GROUPS[q]
        return pl.multiple_of(row + there * (m // 4), 16)

    def ag_copy(q, d, arriving):
        n = GROUPS[q][1] // 4
        at = piece(q, lax.rem(z - d + 4, 4) if arriving else z)
        block = rb.at[c, pl.ds(at, n)]
        return remote(block, block, ag_send.at[q, d - 1], ag_recv.at[q, d - 1], chip(d))

    def far(q):
        return q >= 5

    def s3(q):
        row, m = GROUPS[q]
        n = m // 4
        for d in (1, 2, 3):
            rs_copy(q, d).wait_recv()
        at = pl.ds(piece(q, z), n)
        total = pf[at] + cr[at].astype(jnp.float32)
        for d in (1, 2, 3):
            total = total + rr[d - 1, pl.ds(row // 4, n)].astype(jnp.float32)
        rb[c, at] = total.astype(rb.dtype)
        for d in (2, 1, 3) if far(q) else (1, 3):
            copy = ag_copy(q, d, False)
            copy.start()
            pending.append(copy)

    def fw_copy(q, way, arriving):
        n = GROUPS[q][1] // 4
        first = n // 32 * 16
        start, size = (0, first) if way == 0 else (first, n - first)
        at = piece(q, lax.rem(z + 2, 4) if arriving else lax.rem(z + (3 if way == 0 else 1), 4)) + start
        block = rb.at[c, pl.ds(pl.multiple_of(at, 16), size)]
        return remote(block, block, fw_send.at[q, way], fw_recv.at[q, way], chip(1 if way == 0 else 3))

    def s3b(q):
        if far(q):
            return
        for d, way in ((1, 0), (3, 1)):
            ag_copy(q, d, True).wait_recv()
            copy = fw_copy(q, way, False)
            copy.start()
            pending.append(copy)

    def co_copy(q, arriving):
        row, m = GROUPS[q]
        block = rb.at[1 - c if arriving else c, pl.ds(row, m)]
        return remote(block, block, co_send.at[q], co_recv.at[q], other)

    def s4(q):
        if far(q):
            for d in (1, 2, 3):
                ag_copy(q, d, True).wait_recv()
        else:
            for way in (0, 1):
                fw_copy(q, way, True).wait_recv()
        copy = co_copy(q, False)
        copy.start()
        pending.append(copy)

    def side_of(n):
        return c if n == 0 else 1 - c

    def s5(q, n):
        row, m = GROUPS[q]
        if n == 1:
            co_copy(q, True).wait_recv()
        h = side_of(n)
        for at in range(row // HALF, (row + m) // HALF):
            first = pl.multiple_of(token(*SLOTS[at]), 16)
            length = len_ref[lax.div(first, 4 * HALF)]
            position = lax.broadcasted_iota(jnp.int32, (HALF, half), 0) + lax.rem(first, 4 * HALF)
            block = rb[h, pl.ds(at * HALF, HALF)].astype(jnp.float32)
            rabs[h, pl.ds(first, HALF)] = jnp.where(position < length, block, 0.0).astype(rabs.dtype)

    def az_copy(d, arriving):
        from_z = lax.rem(z - d + 4, 4) if arriving else z
        block = ab.at[:, pl.ds(pl.multiple_of((from_z * 2 + c) * width, 128), width)]
        return remote(block, block, az_send.at[d - 1], az_recv.at[d - 1], chip(d))

    def ac_copy(d, arriving):
        there = lax.rem(z + d, 4) * 2 + (1 - c if arriving else c)
        block = ab.at[:, pl.ds(pl.multiple_of(there * width, 128), width)]
        return remote(block, block, ac_send.at[d], ac_recv.at[d], other)

    def rotate_act():
        for d in range(4):
            ac_copy(d, True).wait_recv()
        w_load.wait()
        first = pl.multiple_of(o * 2 * HALF, 16)
        for start in range(0, width, 256):
            size = min(256, width - start)
            ra[pl.ds(first, 2 * HALF), pl.ds(start, size)] = jnp.dot(
                ab[...], w[:, pl.ds(start, size)], preferred_element_type=jnp.float32
            ).astype(ra.dtype)

    h0 = lax.div(y, 2)
    sequences = [
        x * 2 + h0, x * 2 + 1 - h0,
        lax.rem(x + 1, 4) * 2 + h0, lax.rem(x + 3, 4) * 2 + h0,
        lax.rem(x + 1, 4) * 2 + 1 - h0, lax.rem(x + 3, 4) * 2 + 1 - h0,
        lax.rem(x + 2, 4) * 2 + h0, lax.rem(x + 2, 4) * 2 + 1 - h0,
    ]
    weight_sum = wt_ref[0]
    for n in range(1, 8):
        weight_sum = weight_sum + wt_ref[n]
    weight_sum = weight_sum.astype(jnp.float32)
    def out_copy(n):
        rows = pl.ds(pl.multiple_of(side_of(n) * half, 8), half)
        return pltpu.make_async_copy(acc.at[rows], out_ref.at[rows], out_sem.at[n])

    def final(batch, n):
        h = side_of(n)
        cols = pl.ds(pl.multiple_of(h * half, 8), half)
        for s in batch:
            rows = pl.ds(pl.multiple_of(sequences[s] * 128, 128), 128)
            block = lax.dot_general(
                rabs[h, rows], ra[rows], (((0,), (0,)), ((), ())), preferred_element_type=jnp.float32
            )
            term = wt_ref[sequences[s]].astype(jnp.float32) * block * block
            total = term if s == 0 else acc[cols] + term
            acc[cols] = total / weight_sum if s == 7 else total
        if batch[-1] == 7:
            out_copy(n).start()

    def first_act():
        a_load.wait()
        for d in (2, 1, 3):
            copy = az_copy(d, False)
            copy.start()
            pending.append(copy)

    def swap_act():
        for d in (0, 1, 2, 3):
            if d:
                az_copy(4 - d, True).wait_recv()
            copy = ac_copy(d, False)
            copy.start()
            pending.append(copy)

    g_load.wait()
    issue(0, "1", "2")
    first_act()
    u_load.wait()
    arrive(0, "1")
    issue(0, "3a", "3b", "4b")
    s1(0)
    swap_act()
    s2(0)
    arrive(0, "2")
    issue(0, "5b")
    s1(1)
    arrive(0, "3a")
    issue(0, "6")
    rotate_act()
    s2(1)
    s3(0)
    arrive(0, "3b")
    issue(0, "7a")
    s1(2)
    s2(2)
    s3(1)
    s3b(0)
    arrive(0, "4b")
    issue(0, "7b")
    arrive(0, "5b")
    s1(3)
    s2(3)
    s3(2)
    arrive(0, "6")
    issue(0, "8")
    issue(1, "1", "2")
    s1(4)
    s3b(1)
    s4(0)
    s5(0, 0)
    s2(4)
    arrive(0, "7a", "7b")
    s1(5)
    s3(3)
    s2(5)
    arrive(0, "8")
    s1(6)
    s3b(2)
    s2(6)
    s4(1)
    arrive(1, "1")
    issue(1, "3a", "3b", "4b")
    s3(4)
    arrive(1, "2")
    issue(1, "5b")
    s5(1, 0)
    s5(0, 1)
    s3b(3)
    s5(1, 1)
    arrive(1, "3a")
    issue(1, "6")
    arrive(1, "3b")
    issue(1, "7a")
    s3(5)
    arrive(1, "4b")
    issue(1, "7b")
    s4(2)
    s5(2, 0)
    s3(6)
    s5(2, 1)
    s3b(4)
    s4(3)
    s5(3, 0)
    arrive(1, "5b")
    arrive(1, "6")
    issue(1, "8")
    final((0, 1, 2, 3), 0)
    s5(3, 1)
    final((0, 1, 2, 3), 1)
    s4(5)
    s5(5, 0)
    s4(4)
    s5(4, 0)
    s4(6)
    s5(6, 0)
    arrive(1, "7a", "7b")
    final((4, 5, 6), 0)
    arrive(1, "8")
    final((7,), 0)
    s5(5, 1)
    s5(4, 1)
    s5(6, 1)
    final((4, 5, 6, 7), 1)

    for copy in pending:
        copy.wait_send()
    for n in (0, 1):
        out_copy(n).wait()


def local(activations, act_basis, gradients, grad_basis, lengths, sample_weights):
    rows, wide = gradients.shape
    depth, cols = grad_basis.shape
    full, width = act_basis.shape
    tokens = 16 * rows
    groups = len(GROUPS)
    bf16, f32 = jnp.bfloat16, jnp.float32
    dma = pltpu.SemaphoreType.DMA
    anywhere = pl.BlockSpec(memory_space=pl.ANY)
    scalars = pl.BlockSpec(memory_space=pltpu.SMEM)
    return pl.pallas_call(
        kernel,
        out_shape=jax.ShapeDtypeStruct((cols, width), f32),
        in_specs=[anywhere] * 4 + [scalars] * 2,
        out_specs=anywhere,
        scratch_shapes=[
            pltpu.VMEM((depth, cols), bf16),
            pltpu.VMEM((full, width), bf16),
            pltpu.VMEM((tokens, wide), bf16),
            pltpu.VMEM((tokens, cols // 2), f32),
            pltpu.VMEM((tokens, cols // 2), bf16),
            pltpu.VMEM((tokens, cols // 2), bf16),
            pltpu.VMEM((tokens, cols // 2), bf16),
            pltpu.VMEM((3, tokens // 4, cols // 2), bf16),
            pltpu.VMEM((2, tokens, cols // 2), bf16),
            pltpu.VMEM((2, tokens, cols // 2), bf16),
            pltpu.VMEM((tokens, width), bf16),
            pltpu.VMEM((rows, full), bf16),
            pltpu.VMEM((cols, width), f32),
            dma((4,)),
            dma((2, 40)), dma((2, 40)),
            dma((groups,)), dma((groups,)),
            dma((groups, 3)), dma((groups, 3)),
            dma((groups, 3)), dma((groups, 3)),
            dma((groups, 2)), dma((groups, 2)),
            dma((groups,)), dma((groups,)),
            dma((3,)), dma((3,)),
            dma((4,)), dma((4,)),
            dma((2,)),
        ],
        compiler_params=pltpu.CompilerParams(
            collective_id=0, has_side_effects=True, vmem_limit_bytes=56 * 1024 * 1024
        ),
    )(activations, act_basis, gradients, grad_basis, lengths, sample_weights)


def solution(mesh):
    in_specs = (P("out", "in"), P(None, "in"), P("out", "in"), P("in", "out"), P(), P())
    return jax.shard_map(local, mesh=mesh, in_specs=in_specs, out_specs=P("out", "in"), check_vma=False)
```

```python
import functools

import jax
import jax.numpy as jnp
from jax import lax
from jax.experimental import pallas as pl
from jax.experimental.pallas import tpu as pltpu
from jax.sharding import PartitionSpec as P

MESH = pl.DeviceIdType.MESH
HALF = 32
STAGES = ("own", "1", "2", "3a", "3b", "4b", "5b", "6", "7a", "7b", "8")
BRINGS = {
    "own": [(0, 0)],
    "1": [(1, 0), (-1, 0)],
    "2": [(0, 1), (0, -1)],
    "3a": [(2, 0)],
    "3b": [(1, 1), (1, -1)],
    "4b": [(-1, 1), (-1, -1)],
    "5b": [(0, 2)],
    "6": [(2, 1), (2, -1)],
    "7a": [(1, 2)],
    "7b": [(-1, 2)],
    "8": [(2, 2)],
}
SLOTS = [(lane, a, b) for stage in STAGES for lane in (0, 1) for a, b in BRINGS[stage]]
OFFSET = {slot: HALF * at for at, slot in enumerate(SLOTS)}
GROUPS = [(0, 192), (192, 128), (320, 192), (512, 192), (704, 128), (832, 128), (960, 64)]


def moves(stage):
    found = []
    for lane in (0, 1):
        for sign in (1, -1):
            part = 1 if sign == 1 else 2
            one = {
                "1": ((0, 0), (-sign, 0), 0, 0),
                "2": ((0, 0), (0, -sign), 1, 0),
                "3a": ((-sign, 0), (2, 0), 0, part),
                "3b": ((1, 0), (1, -sign), 1, 0),
                "4b": ((-1, 0), (-1, -sign), 1, 0),
                "5b": ((0, -sign), (0, 2), 1, part),
                "6": ((2, 0), (2, -sign), 1, 0),
                "7a": ((1, -sign), (1, 2), 1, part),
                "7b": ((-1, -sign), (-1, 2), 1, part),
                "8": ((2, -sign), (2, 2), 1, part),
            }[stage]
            found.append((lane, one[0], one[1], one[2], sign, one[3]))
    return found


def rows_of(part):
    return (0, HALF) if part == 0 else ((0, HALF // 2) if part == 1 else (HALF // 2, HALF // 2))


def kernel(
    act_ref, w_ref, g_ref, u_ref, len_hbm, wt_hbm, out_ref,
    u, w, gb, pf, cs, cr, sb, rr, rb, rabs, ra, ab, acc, len_ref, wt_ref,
    load_sem, xy_send, xy_recv, core_send, core_recv, rs_send, rs_recv,
    ag_send, ag_recv, fw_send, fw_recv, co_send, co_recv, az_send, az_recv, ac_send, ac_recv, out_sem,
):
    i, o = lax.axis_index("in"), lax.axis_index("out")
    z, c = lax.div(i, 2), lax.rem(i, 2)
    x, y = lax.div(o, 4), lax.rem(o, 4)
    width = ra.shape[1]
    half = rb.shape[2]

    def xy(axis, sign):
        if axis == 0:
            return (i, lax.rem(x + sign + 4, 4) * 4 + y)
        return (i, x * 4 + lax.rem(y + sign + 4, 4))

    def chip(d):
        return (lax.rem(z + d, 4) * 2 + c, o)

    other = (z * 2 + 1 - c, o)
    pending = []

    g_load = pltpu.make_async_copy(g_ref, gb.at[pl.ds(0, 2 * HALF)], load_sem.at[0])
    mine = pl.ds(pl.multiple_of(i * width, 128), width)
    a_load = pltpu.make_async_copy(act_ref, ab.at[:, mine], load_sem.at[1])
    u_load = pltpu.make_async_copy(u_ref, u, load_sem.at[2])
    w_load = pltpu.make_async_copy(w_ref, w, load_sem.at[3])
    len_load = pltpu.make_async_copy(len_hbm, len_ref, load_sem.at[4])
    wt_load = pltpu.make_async_copy(wt_hbm, wt_ref, load_sem.at[5])
    for load in (g_load, a_load, u_load, w_load, len_load, wt_load):
        load.start()

    peers = [xy(0, 1), xy(0, -1), xy(1, 1), xy(1, -1), chip(1), chip(2), chip(3), other]
    barrier = pltpu.get_barrier_semaphore()
    for peer in peers:
        pl.semaphore_signal(barrier, inc=1, device_id=peer, device_id_type=MESH)
    pl.semaphore_wait(barrier, len(peers))

    def remote(src, dst, send, recv, device):
        return pltpu.make_async_remote_copy(
            src_ref=src, dst_ref=dst, send_sem=send, recv_sem=recv, device_id=device, device_id_type=MESH
        )

    def token(lane, a, b):
        dx, dy = (b, a) if lane == 0 else (a, b)
        shard = lax.rem(x + dx + 4, 4) * 4 + lax.rem(y + dy + 4, 4)
        return shard * 2 * HALF + lane * HALF

    def xy_copy(kind, stage, at, arriving):
        lane, src, dst, axis, sign, part = moves(stage)[at]
        number = 4 * STAGES.index(stage) - 4 + at
        start, size = rows_of(part)
        if kind == 0:
            from_row, to_row, ref = OFFSET[(lane, *src)] + start, OFFSET[(lane, *dst)] + start, gb
        else:
            ref = ra
            from_row = pl.multiple_of(token(lane, *src) + start, 16)
            to_row = pl.multiple_of(token(lane, *dst) + start, 16) if arriving else from_row
        return remote(
            ref.at[pl.ds(from_row, size)], ref.at[pl.ds(to_row, size)],
            xy_send.at[kind, number], xy_recv.at[kind, number],
            xy(1 - axis if lane == 0 else axis, sign),
        )

    def issue(kind, *stages, start=True, record=True):
        for stage in stages:
            for at in range(4):
                copy = xy_copy(kind, stage, at, False)
                if start:
                    copy.start()
                if record:
                    pending.append(copy)

    def arrive(kind, *stages):
        for stage in stages:
            for at in range(4):
                xy_copy(kind, stage, at, True).wait_recv()

    def core_copy(q):
        row, m = GROUPS[q]
        return remote(cs.at[pl.ds(row, m)], cr.at[pl.ds(row, m)], core_send.at[q], core_recv.at[q], other)

    def s1(q, between=None):
        row, m = GROUPS[q]
        rows = pl.ds(row, m)

        def side(n, carry):
            cols = pl.ds(pl.multiple_of(lax.rem(1 - c + n, 2) * half, 128), half)
            pf[rows] = jnp.dot(gb[rows], u[:, cols], preferred_element_type=jnp.float32)

            @pl.when(n == 0)
            def _():
                cs[rows] = pf[rows].astype(cs.dtype)
                core_copy(q).start()
                if between is not None:
                    between()

            return carry

        lax.fori_loop(0, 2, side, 0)
        pending.append(core_copy(q))

    def rs_copy(q, d):
        row, m = GROUPS[q]
        n = m // 4
        there = lax.rem(z + d, 4)
        return remote(
            sb.at[pl.ds(pl.multiple_of(row + there * n, 16), n)], rr.at[d - 1, pl.ds(row // 4, n)],
            rs_send.at[q, d - 1], rs_recv.at[q, d - 1], chip(d),
        )

    def s2(q):
        row, m = GROUPS[q]
        core_copy(q).wait_recv()
        sb[pl.ds(row, m)] = (pf[pl.ds(row, m)] + cr[pl.ds(row, m)].astype(jnp.float32)).astype(sb.dtype)
        for d in (2, 1, 3):
            copy = rs_copy(q, d)
            copy.start()
            pending.append(copy)

    def piece(q, there):
        row, m = GROUPS[q]
        return pl.multiple_of(row + there * (m // 4), 16)

    def ag_copy(q, d, arriving):
        n = GROUPS[q][1] // 4
        at = piece(q, lax.rem(z - d + 4, 4) if arriving else z)
        block = rb.at[c, pl.ds(at, n)]
        return remote(block, block, ag_send.at[q, d - 1], ag_recv.at[q, d - 1], chip(d))

    def far(q):
        return q >= 5

    def s3(q):
        row, m = GROUPS[q]
        n = m // 4
        for d in (1, 2, 3):
            rs_copy(q, d).wait_recv()
        at = pl.ds(piece(q, z), n)
        total = pf[at] + cr[at].astype(jnp.float32)
        for d in (1, 2, 3):
            total = total + rr[d - 1, pl.ds(row // 4, n)].astype(jnp.float32)
        rb[c, at] = total.astype(rb.dtype)
        for d in (2, 1, 3) if far(q) else (1, 3):
            copy = ag_copy(q, d, False)
            copy.start()
            pending.append(copy)

    def fw_copy(q, way, arriving):
        n = GROUPS[q][1] // 4
        first = n // 32 * 16
        start, size = (0, first) if way == 0 else (first, n - first)
        at = piece(q, lax.rem(z + 2, 4) if arriving else lax.rem(z + (3 if way == 0 else 1), 4)) + start
        block = rb.at[c, pl.ds(pl.multiple_of(at, 16), size)]
        return remote(block, block, fw_send.at[q, way], fw_recv.at[q, way], chip(1 if way == 0 else 3))

    def s3b(q):
        if far(q):
            return
        for d, way in ((1, 0), (3, 1)):
            ag_copy(q, d, True).wait_recv()
            copy = fw_copy(q, way, False)
            copy.start()
            pending.append(copy)

    def co_copy(q, arriving):
        row, m = GROUPS[q]
        block = rb.at[1 - c if arriving else c, pl.ds(row, m)]
        return remote(block, block, co_send.at[q], co_recv.at[q], other)

    def s4(q):
        if far(q):
            for d in (1, 2, 3):
                ag_copy(q, d, True).wait_recv()
        else:
            for way in (0, 1):
                fw_copy(q, way, True).wait_recv()
        copy = co_copy(q, False)
        copy.start()
        pending.append(copy)

    def side_of(n):
        return c if n == 0 else 1 - c

    def s5(q, n):
        row, m = GROUPS[q]
        if n == 1:
            co_copy(q, True).wait_recv()
        h = side_of(n)
        for at in range(row // HALF, (row + m) // HALF):
            first = pl.multiple_of(token(*SLOTS[at]), 16)
            length = len_ref[lax.div(first, 4 * HALF)]
            position = lax.broadcasted_iota(jnp.int32, (HALF, half), 0) + lax.rem(first, 4 * HALF)
            block = rb[h, pl.ds(at * HALF, HALF)].astype(jnp.float32)
            rabs[h, pl.ds(first, HALF)] = jnp.where(position < length, block, 0.0).astype(rabs.dtype)

    def az_copy(d, arriving):
        from_z = lax.rem(z - d + 4, 4) if arriving else z
        block = ab.at[:, pl.ds(pl.multiple_of((from_z * 2 + c) * width, 128), width)]
        return remote(block, block, az_send.at[d - 1], az_recv.at[d - 1], chip(d))

    def ac_copy(d, arriving):
        there = lax.rem(z + d, 4) * 2 + (1 - c if arriving else c)
        block = ab.at[:, pl.ds(pl.multiple_of(there * width, 128), width)]
        return remote(block, block, ac_send.at[d], ac_recv.at[d], other)

    def rotate_act():
        for d in range(4):
            ac_copy(d, True).wait_recv()
        w_load.wait()
        first = pl.multiple_of(o * 2 * HALF, 16)
        for start in range(0, width, 256):
            size = min(256, width - start)
            ra[pl.ds(first, 2 * HALF), pl.ds(start, size)] = jnp.dot(
                ab[...], w[:, pl.ds(start, size)], preferred_element_type=jnp.float32
            ).astype(ra.dtype)

    h0 = lax.div(y, 2)
    sequences = [
        x * 2 + h0, x * 2 + 1 - h0,
        lax.rem(x + 1, 4) * 2 + h0, lax.rem(x + 3, 4) * 2 + h0,
        lax.rem(x + 1, 4) * 2 + 1 - h0, lax.rem(x + 3, 4) * 2 + 1 - h0,
        lax.rem(x + 2, 4) * 2 + h0, lax.rem(x + 2, 4) * 2 + 1 - h0,
    ]
    def weight_sum():
        total = wt_ref[0]
        for n in range(1, 8):
            total = total + wt_ref[n]
        return total.astype(jnp.float32)

    pieces = [(0, 0, half), (1, 0, 256), (1, 256, 256), (1, 512, half - 512)]

    def out_copy(number):
        n, start, size = pieces[number]
        rows = pl.ds(pl.multiple_of(side_of(n) * half + start, 8), size)
        return pltpu.make_async_copy(acc.at[rows], out_ref.at[rows], out_sem.at[number])

    def final(batch, n):
        last = batch[-1] == 7
        h = side_of(n)
        for number, (side, start, size) in enumerate(pieces if last else [(n, 0, half)]):
            if side != n:
                continue
            out = pl.ds(pl.multiple_of(h * half + start, 8), size)
            for s in batch:
                rows = pl.ds(pl.multiple_of(sequences[s] * 128, 128), 128)
                block = lax.dot_general(
                    rabs[h, rows, pl.ds(start, size)], ra[rows], (((0,), (0,)), ((), ())),
                    preferred_element_type=jnp.float32,
                )
                term = wt_ref[sequences[s]].astype(jnp.float32) * block * block
                total = term if s == 0 else acc[out] + term
                acc[out] = total / weight_sum() if s == 7 else total
            if last:
                out_copy(number).start()

    def first_act():
        a_load.wait()
        for d in (2, 1, 3):
            copy = az_copy(d, False)
            copy.start()
            pending.append(copy)

    def swap_act():
        for d in (0, 1, 2, 3):
            if d:
                az_copy(4 - d, True).wait_recv()
            copy = ac_copy(d, False)
            copy.start()
            pending.append(copy)

    g_load.wait()
    issue(0, "1", "2")
    first_act()
    u_load.wait()
    arrive(0, "1")
    issue(0, "3a", "3b", "4b")
    s1(0)
    swap_act()
    s2(0)
    arrive(0, "2")
    issue(0, "5b")
    s1(1)
    arrive(0, "3a")
    issue(0, "6")
    rotate_act()
    s2(1)
    s3(0)
    arrive(0, "3b")
    issue(0, "7a")
    s1(2)
    s2(2)
    s3(1)
    s3b(0)
    arrive(0, "4b")
    issue(0, "7b")
    arrive(0, "5b")
    s1(3)
    s2(3)
    s3(2)
    arrive(0, "6")
    issue(0, "8")
    issue(1, "1", "2")
    s1(4)
    s3b(1)
    len_load.wait()
    wt_load.wait()
    s4(0)
    s5(0, 0)
    s2(4)
    arrive(0, "7a", "7b")
    s1(5)
    s3(3)
    s2(5)
    arrive(0, "8")
    s1(6)
    s3b(2)
    s2(6)
    s4(1)
    arrive(1, "1")
    issue(1, "3a", "3b", "4b")
    s3(4)
    arrive(1, "2")
    issue(1, "5b")
    s5(1, 0)
    s5(0, 1)
    s3b(3)
    s5(1, 1)
    arrive(1, "3a")
    issue(1, "6")
    arrive(1, "3b")
    issue(1, "7a")
    s3(5)
    arrive(1, "4b")
    issue(1, "7b")
    s4(2)
    s5(2, 0)
    s3(6)
    s5(2, 1)
    s3b(4)
    s4(3)
    s5(3, 0)
    arrive(1, "5b")
    arrive(1, "6")
    issue(1, "8")
    final((0, 1, 2, 3), 0)
    s5(3, 1)
    final((0, 1, 2, 3), 1)
    s4(5)
    s5(5, 0)
    s4(4)
    s5(4, 0)
    s4(6)
    s5(6, 0)
    arrive(1, "7a", "7b")
    final((4, 5, 6), 0)
    arrive(1, "8")
    final((7,), 0)
    s5(5, 1)
    s5(4, 1)
    s5(6, 1)
    final((4, 5, 6), 1)
    final((7,), 1)

    for copy in pending:
        copy.wait_send()
    for number in range(len(pieces)):
        out_copy(number).wait()


def local(activations, act_basis, gradients, grad_basis, lengths, sample_weights):
    rows, wide = gradients.shape
    depth, cols = grad_basis.shape
    full, width = act_basis.shape
    tokens = 16 * rows
    groups = len(GROUPS)
    bf16, f32 = jnp.bfloat16, jnp.float32
    dma = pltpu.SemaphoreType.DMA
    anywhere = pl.BlockSpec(memory_space=pl.ANY)
    return pl.pallas_call(
        kernel,
        out_shape=jax.ShapeDtypeStruct((cols, width), f32),
        in_specs=[anywhere] * 6,
        out_specs=anywhere,
        scratch_shapes=[
            pltpu.VMEM((depth, cols), bf16),
            pltpu.VMEM((full, width), bf16),
            pltpu.VMEM((tokens, wide), bf16),
            pltpu.VMEM((tokens, cols // 2), f32),
            pltpu.VMEM((tokens, cols // 2), bf16),
            pltpu.VMEM((tokens, cols // 2), bf16),
            pltpu.VMEM((tokens, cols // 2), bf16),
            pltpu.VMEM((3, tokens // 4, cols // 2), bf16),
            pltpu.VMEM((2, tokens, cols // 2), bf16),
            pltpu.VMEM((2, tokens, cols // 2), bf16),
            pltpu.VMEM((tokens, width), bf16),
            pltpu.VMEM((rows, full), bf16),
            pltpu.VMEM((cols, width), f32),
            pltpu.SMEM((8,), jnp.int32),
            pltpu.SMEM((8,), jnp.int32),
            dma((6,)),
            dma((2, 40)), dma((2, 40)),
            dma((groups,)), dma((groups,)),
            dma((groups, 3)), dma((groups, 3)),
            dma((groups, 3)), dma((groups, 3)),
            dma((groups, 2)), dma((groups, 2)),
            dma((groups,)), dma((groups,)),
            dma((3,)), dma((3,)),
            dma((4,)), dma((4,)),
            dma((4,)),
        ],
        compiler_params=pltpu.CompilerParams(
            collective_id=0, has_side_effects=True, vmem_limit_bytes=56 * 1024 * 1024
        ),
    )(activations, act_basis, gradients, grad_basis, lengths, sample_weights)


def solution(mesh):
    in_specs = (P("out", "in"), P(None, "in"), P("out", "in"), P("in", "out"), P(), P())
    return jax.shard_map(local, mesh=mesh, in_specs=in_specs, out_specs=P("out", "in"), check_vma=False)
```

```python
import functools

import jax
import jax.numpy as jnp
from jax import lax
from jax.experimental import pallas as pl
from jax.experimental.pallas import tpu as pltpu
from jax.sharding import PartitionSpec as P

MESH = pl.DeviceIdType.MESH
HALF = 32
STAGES = ("own", "1", "2", "3a", "3b", "4b", "5b", "6", "7a", "7b", "8")
BRINGS = {
    "own": [(0, 0)],
    "1": [(1, 0), (-1, 0)],
    "2": [(0, 1), (0, -1)],
    "3a": [(2, 0)],
    "3b": [(1, 1), (1, -1)],
    "4b": [(-1, 1), (-1, -1)],
    "5b": [(0, 2)],
    "6": [(2, 1), (2, -1)],
    "7a": [(1, 2)],
    "7b": [(-1, 2)],
    "8": [(2, 2)],
}
SLOTS = [(lane, a, b) for stage in STAGES for lane in (0, 1) for a, b in BRINGS[stage]]
OFFSET = {slot: HALF * at for at, slot in enumerate(SLOTS)}
GROUPS = [(0, 64), (64, 128), (192, 128), (320, 192), (512, 192), (704, 128), (832, 128), (960, 64)]


def moves(stage):
    found = []
    for lane in (0, 1):
        for sign in (1, -1):
            part = 1 if sign == 1 else 2
            one = {
                "1": ((0, 0), (-sign, 0), 0, 0),
                "2": ((0, 0), (0, -sign), 1, 0),
                "3a": ((-sign, 0), (2, 0), 0, part),
                "3b": ((1, 0), (1, -sign), 1, 0),
                "4b": ((-1, 0), (-1, -sign), 1, 0),
                "5b": ((0, -sign), (0, 2), 1, part),
                "6": ((2, 0), (2, -sign), 1, 0),
                "7a": ((1, -sign), (1, 2), 1, part),
                "7b": ((-1, -sign), (-1, 2), 1, part),
                "8": ((2, -sign), (2, 2), 1, part),
            }[stage]
            found.append((lane, one[0], one[1], one[2], sign, one[3]))
    return found


def rows_of(part):
    return (0, HALF) if part == 0 else ((0, HALF // 2) if part == 1 else (HALF // 2, HALF // 2))


def kernel(
    act_ref, w_ref, g_ref, u_ref, len_hbm, wt_hbm, out_ref,
    u, w, gb, pf, cs, cr, sb, rr, rb, rabs, ra, ab, acc, len_ref, wt_ref,
    load_sem, xy_send, xy_recv, core_send, core_recv, rs_send, rs_recv,
    ag_send, ag_recv, fw_send, fw_recv, co_send, co_recv, az_send, az_recv, ac_send, ac_recv, out_sem,
):
    i, o = lax.axis_index("in"), lax.axis_index("out")
    z, c = lax.div(i, 2), lax.rem(i, 2)
    x, y = lax.div(o, 4), lax.rem(o, 4)
    width = ra.shape[1]
    half = rb.shape[2]

    def xy(axis, sign):
        if axis == 0:
            return (i, lax.rem(x + sign + 4, 4) * 4 + y)
        return (i, x * 4 + lax.rem(y + sign + 4, 4))

    def chip(d):
        return (lax.rem(z + d, 4) * 2 + c, o)

    other = (z * 2 + 1 - c, o)
    pending = []

    g_load = pltpu.make_async_copy(g_ref, gb.at[pl.ds(0, 2 * HALF)], load_sem.at[0])
    mine = pl.ds(pl.multiple_of(i * width, 128), width)
    a_load = pltpu.make_async_copy(act_ref, ab.at[:, mine], load_sem.at[1])
    u_load = pltpu.make_async_copy(u_ref, u, load_sem.at[2])
    w_load = pltpu.make_async_copy(w_ref, w, load_sem.at[3])
    len_load = pltpu.make_async_copy(len_hbm, len_ref, load_sem.at[4])
    wt_load = pltpu.make_async_copy(wt_hbm, wt_ref, load_sem.at[5])
    for load in (g_load, a_load, u_load, len_load, wt_load):
        load.start()

    peers = [xy(0, 1), xy(0, -1), xy(1, 1), xy(1, -1), chip(1), chip(2), chip(3), other]
    barrier = pltpu.get_barrier_semaphore()
    for peer in peers:
        pl.semaphore_signal(barrier, inc=1, device_id=peer, device_id_type=MESH)
    pl.semaphore_wait(barrier, len(peers))

    def remote(src, dst, send, recv, device):
        return pltpu.make_async_remote_copy(
            src_ref=src, dst_ref=dst, send_sem=send, recv_sem=recv, device_id=device, device_id_type=MESH
        )

    def token(lane, a, b):
        dx, dy = (b, a) if lane == 0 else (a, b)
        shard = lax.rem(x + dx + 4, 4) * 4 + lax.rem(y + dy + 4, 4)
        return shard * 2 * HALF + lane * HALF

    def xy_copy(kind, stage, at, arriving):
        lane, src, dst, axis, sign, part = moves(stage)[at]
        number = 4 * STAGES.index(stage) - 4 + at
        start, size = rows_of(part)
        if kind == 0:
            from_row, to_row, ref = OFFSET[(lane, *src)] + start, OFFSET[(lane, *dst)] + start, gb
        else:
            ref = ra
            from_row = pl.multiple_of(token(lane, *src) + start, 16)
            to_row = pl.multiple_of(token(lane, *dst) + start, 16) if arriving else from_row
        return remote(
            ref.at[pl.ds(from_row, size)], ref.at[pl.ds(to_row, size)],
            xy_send.at[kind, number], xy_recv.at[kind, number],
            xy(1 - axis if lane == 0 else axis, sign),
        )

    def issue(kind, *stages, start=True, record=True):
        for stage in stages:
            for at in range(4):
                copy = xy_copy(kind, stage, at, False)
                if start:
                    copy.start()
                if record:
                    pending.append(copy)

    def arrive(kind, *stages):
        for stage in stages:
            for at in range(4):
                xy_copy(kind, stage, at, True).wait_recv()

    def core_copy(q):
        row, m = GROUPS[q]
        return remote(cs.at[pl.ds(row, m)], cr.at[pl.ds(row, m)], core_send.at[q], core_recv.at[q], other)

    def s1(q, between=None):
        row, m = GROUPS[q]
        rows = pl.ds(row, m)

        def side(n, carry):
            cols = pl.ds(pl.multiple_of(lax.rem(1 - c + n, 2) * half, 128), half)
            pf[rows] = jnp.dot(gb[rows], u[:, cols], preferred_element_type=jnp.float32)

            @pl.when(n == 0)
            def _():
                cs[rows] = pf[rows].astype(cs.dtype)
                core_copy(q).start()
                if between is not None:
                    between()

            return carry

        lax.fori_loop(0, 2, side, 0)
        pending.append(core_copy(q))

    def rs_copy(q, d):
        row, m = GROUPS[q]
        n = m // 4
        there = lax.rem(z + d, 4)
        return remote(
            sb.at[pl.ds(pl.multiple_of(row + there * n, 16), n)], rr.at[d - 1, pl.ds(row // 4, n)],
            rs_send.at[q, d - 1], rs_recv.at[q, d - 1], chip(d),
        )

    def s2(q):
        row, m = GROUPS[q]
        core_copy(q).wait_recv()
        sb[pl.ds(row, m)] = (pf[pl.ds(row, m)] + cr[pl.ds(row, m)].astype(jnp.float32)).astype(sb.dtype)
        for d in (2, 1, 3):
            copy = rs_copy(q, d)
            copy.start()
            pending.append(copy)

    def piece(q, there):
        row, m = GROUPS[q]
        return pl.multiple_of(row + there * (m // 4), 16)

    def ag_copy(q, d, arriving):
        n = GROUPS[q][1] // 4
        at = piece(q, lax.rem(z - d + 4, 4) if arriving else z)
        block = rb.at[c, pl.ds(at, n)]
        return remote(block, block, ag_send.at[q, d - 1], ag_recv.at[q, d - 1], chip(d))

    def far(q):
        return q >= 6 or q == 0

    def s3(q):
        row, m = GROUPS[q]
        n = m // 4
        for d in (1, 2, 3):
            rs_copy(q, d).wait_recv()
        at = pl.ds(piece(q, z), n)
        total = pf[at] + cr[at].astype(jnp.float32)
        for d in (1, 2, 3):
            total = total + rr[d - 1, pl.ds(row // 4, n)].astype(jnp.float32)
        rb[c, at] = total.astype(rb.dtype)
        for d in (2, 1, 3) if far(q) else (1, 3):
            copy = ag_copy(q, d, False)
            copy.start()
            pending.append(copy)

    def fw_copy(q, way, arriving):
        n = GROUPS[q][1] // 4
        first = n // 32 * 16
        start, size = (0, first) if way == 0 else (first, n - first)
        at = piece(q, lax.rem(z + 2, 4) if arriving else lax.rem(z + (3 if way == 0 else 1), 4)) + start
        block = rb.at[c, pl.ds(pl.multiple_of(at, 16), size)]
        return remote(block, block, fw_send.at[q, way], fw_recv.at[q, way], chip(1 if way == 0 else 3))

    def s3b(q):
        if far(q):
            return
        for d, way in ((1, 0), (3, 1)):
            ag_copy(q, d, True).wait_recv()
            copy = fw_copy(q, way, False)
            copy.start()
            pending.append(copy)

    def co_copy(q, arriving):
        row, m = GROUPS[q]
        block = rb.at[1 - c if arriving else c, pl.ds(row, m)]
        return remote(block, block, co_send.at[q], co_recv.at[q], other)

    def s4(q):
        if far(q):
            for d in (1, 2, 3):
                ag_copy(q, d, True).wait_recv()
        else:
            for way in (0, 1):
                fw_copy(q, way, True).wait_recv()
        copy = co_copy(q, False)
        copy.start()
        pending.append(copy)

    def side_of(n):
        return c if n == 0 else 1 - c

    def s5(q, n):
        row, m = GROUPS[q]
        if n == 1:
            co_copy(q, True).wait_recv()
        h = side_of(n)
        for at in range(row // HALF, (row + m) // HALF):
            first = pl.multiple_of(token(*SLOTS[at]), 16)
            length = len_ref[lax.div(first, 4 * HALF)]
            position = lax.broadcasted_iota(jnp.int32, (HALF, half), 0) + lax.rem(first, 4 * HALF)
            block = rb[h, pl.ds(at * HALF, HALF)].astype(jnp.float32)
            rabs[h, pl.ds(first, HALF)] = jnp.where(position < length, block, 0.0).astype(rabs.dtype)

    def az_copy(d, arriving):
        from_z = lax.rem(z - d + 4, 4) if arriving else z
        block = ab.at[:, pl.ds(pl.multiple_of((from_z * 2 + c) * width, 128), width)]
        return remote(block, block, az_send.at[d - 1], az_recv.at[d - 1], chip(d))

    def ac_copy(d, arriving):
        there = lax.rem(z + d, 4) * 2 + (1 - c if arriving else c)
        block = ab.at[:, pl.ds(pl.multiple_of(there * width, 128), width)]
        return remote(block, block, ac_send.at[d], ac_recv.at[d], other)

    def rotate_act():
        for d in range(4):
            ac_copy(d, True).wait_recv()
        w_load.wait()
        first = pl.multiple_of(o * 2 * HALF, 16)
        for start in range(0, width, 256):
            size = min(256, width - start)
            ra[pl.ds(first, 2 * HALF), pl.ds(start, size)] = jnp.dot(
                ab[...], w[:, pl.ds(start, size)], preferred_element_type=jnp.float32
            ).astype(ra.dtype)

    h0 = lax.div(y, 2)
    sequences = [
        x * 2 + h0, x * 2 + 1 - h0,
        lax.rem(x + 1, 4) * 2 + h0, lax.rem(x + 3, 4) * 2 + h0,
        lax.rem(x + 1, 4) * 2 + 1 - h0, lax.rem(x + 3, 4) * 2 + 1 - h0,
        lax.rem(x + 2, 4) * 2 + h0, lax.rem(x + 2, 4) * 2 + 1 - h0,
    ]
    def weight_sum():
        total = wt_ref[0]
        for n in range(1, 8):
            total = total + wt_ref[n]
        return total.astype(jnp.float32)

    pieces = [(0, 0, half), (1, 0, 256), (1, 256, 256), (1, 512, half - 512)]

    def out_copy(number):
        n, start, size = pieces[number]
        rows = pl.ds(pl.multiple_of(side_of(n) * half + start, 8), size)
        return pltpu.make_async_copy(acc.at[rows], out_ref.at[rows], out_sem.at[number])

    def final(batch, n):
        last = batch[-1] == 7
        h = side_of(n)
        for number, (side, start, size) in enumerate(pieces if last else [(n, 0, half)]):
            if side != n:
                continue
            out = pl.ds(pl.multiple_of(h * half + start, 8), size)
            for s in batch:
                rows = pl.ds(pl.multiple_of(sequences[s] * 128, 128), 128)
                block = lax.dot_general(
                    rabs[h, rows, pl.ds(start, size)], ra[rows], (((0,), (0,)), ((), ())),
                    preferred_element_type=jnp.float32,
                )
                term = wt_ref[sequences[s]].astype(jnp.float32) * block * block
                total = term if s == 0 else acc[out] + term
                acc[out] = total / weight_sum() if s == 7 else total
            if last:
                out_copy(number).start()

    def first_act():
        a_load.wait()
        for d in (2, 1, 3):
            copy = az_copy(d, False)
            copy.start()
            pending.append(copy)

    def swap_act():
        for d in (0, 1, 2, 3):
            if d:
                az_copy(4 - d, True).wait_recv()
            copy = ac_copy(d, False)
            copy.start()
            pending.append(copy)

    g_load.wait()
    issue(0, "1", "2")
    first_act()
    u_load.wait()
    w_load.start()
    s1(0)
    s2(0)
    arrive(0, "1")
    issue(0, "3a", "3b", "4b")
    s1(1)
    swap_act()
    s3(0)
    s2(1)
    arrive(0, "2")
    issue(0, "5b")
    s1(2)
    arrive(0, "3a")
    issue(0, "6")
    rotate_act()
    s4(0)
    s2(2)
    s3(1)
    arrive(0, "3b")
    issue(0, "7a")
    s1(3)
    s2(3)
    s3(2)
    s3b(1)
    arrive(0, "4b")
    issue(0, "7b")
    arrive(0, "5b")
    s1(4)
    s2(4)
    s3(3)
    arrive(0, "6")
    issue(0, "8")
    issue(1, "1", "2")
    s1(5)
    s3b(2)
    s4(1)
    len_load.wait()
    wt_load.wait()
    s5(0, 0)
    s5(0, 1)
    s5(1, 0)
    s2(5)
    arrive(0, "7a", "7b")
    s1(6)
    s3(4)
    s2(6)
    arrive(0, "8")
    s1(7)
    s3b(3)
    s2(7)
    s4(2)
    arrive(1, "1")
    issue(1, "3a", "3b", "4b")
    s3(5)
    arrive(1, "2")
    issue(1, "5b")
    s5(2, 0)
    s5(1, 1)
    s3b(4)
    s5(2, 1)
    arrive(1, "3a")
    issue(1, "6")
    arrive(1, "3b")
    issue(1, "7a")
    s3(6)
    arrive(1, "4b")
    issue(1, "7b")
    s4(3)
    s5(3, 0)
    s3(7)
    s5(3, 1)
    s3b(5)
    s4(4)
    s5(4, 0)
    arrive(1, "5b")
    arrive(1, "6")
    issue(1, "8")
    final((0, 1, 2, 3), 0)
    s5(4, 1)
    final((0, 1, 2, 3), 1)
    s4(6)
    s5(6, 0)
    s4(5)
    s5(5, 0)
    s4(7)
    s5(7, 0)
    arrive(1, "7a", "7b")
    final((4, 5, 6), 0)
    arrive(1, "8")
    final((7,), 0)
    s5(6, 1)
    s5(5, 1)
    s5(7, 1)
    final((4, 5, 6), 1)
    final((7,), 1)

    for copy in pending:
        copy.wait_send()
    for number in range(len(pieces)):
        out_copy(number).wait()


def local(activations, act_basis, gradients, grad_basis, lengths, sample_weights):
    rows, wide = gradients.shape
    depth, cols = grad_basis.shape
    full, width = act_basis.shape
    tokens = 16 * rows
    groups = len(GROUPS)
    bf16, f32 = jnp.bfloat16, jnp.float32
    dma = pltpu.SemaphoreType.DMA
    anywhere = pl.BlockSpec(memory_space=pl.ANY)
    return pl.pallas_call(
        kernel,
        out_shape=jax.ShapeDtypeStruct((cols, width), f32),
        in_specs=[anywhere] * 6,
        out_specs=anywhere,
        scratch_shapes=[
            pltpu.VMEM((depth, cols), bf16),
            pltpu.VMEM((full, width), bf16),
            pltpu.VMEM((tokens, wide), bf16),
            pltpu.VMEM((tokens, cols // 2), f32),
            pltpu.VMEM((tokens, cols // 2), bf16),
            pltpu.VMEM((tokens, cols // 2), bf16),
            pltpu.VMEM((tokens, cols // 2), bf16),
            pltpu.VMEM((3, tokens // 4, cols // 2), bf16),
            pltpu.VMEM((2, tokens, cols // 2), bf16),
            pltpu.VMEM((2, tokens, cols // 2), bf16),
            pltpu.VMEM((tokens, width), bf16),
            pltpu.VMEM((rows, full), bf16),
            pltpu.VMEM((cols, width), f32),
            pltpu.SMEM((8,), jnp.int32),
            pltpu.SMEM((8,), jnp.int32),
            dma((6,)),
            dma((2, 40)), dma((2, 40)),
            dma((groups,)), dma((groups,)),
            dma((groups, 3)), dma((groups, 3)),
            dma((groups, 3)), dma((groups, 3)),
            dma((groups, 2)), dma((groups, 2)),
            dma((groups,)), dma((groups,)),
            dma((3,)), dma((3,)),
            dma((4,)), dma((4,)),
            dma((4,)),
        ],
        compiler_params=pltpu.CompilerParams(
            collective_id=0, has_side_effects=True, vmem_limit_bytes=56 * 1024 * 1024
        ),
    )(activations, act_basis, gradients, grad_basis, lengths, sample_weights)


def solution(mesh):
    in_specs = (P("out", "in"), P(None, "in"), P("out", "in"), P("in", "out"), P(), P())
    return jax.shard_map(local, mesh=mesh, in_specs=in_specs, out_specs=P("out", "in"), check_vma=False)
```

```python
import functools

import jax
import jax.numpy as jnp
from jax import lax
from jax.experimental import pallas as pl
from jax.experimental.pallas import tpu as pltpu
from jax.sharding import PartitionSpec as P

MESH = pl.DeviceIdType.MESH
HALF = 32
STAGES = ("own", "1", "2", "3a", "3b", "4b", "5b", "6", "7a", "7b", "8")
BRINGS = {
    "own": [(0, 0)],
    "1": [(1, 0), (-1, 0)],
    "2": [(0, 1), (0, -1)],
    "3a": [(2, 0)],
    "3b": [(1, 1), (1, -1)],
    "4b": [(-1, 1), (-1, -1)],
    "5b": [(0, 2)],
    "6": [(2, 1), (2, -1)],
    "7a": [(1, 2)],
    "7b": [(-1, 2)],
    "8": [(2, 2)],
}
SLOTS = [(lane, a, b) for stage in STAGES for lane in (0, 1) for a, b in BRINGS[stage]]
OFFSET = {slot: HALF * at for at, slot in enumerate(SLOTS)}
GROUPS = [(0, 192), (192, 128), (320, 192), (512, 192), (704, 128), (832, 128), (960, 64)]


def moves(stage):
    found = []
    for lane in (0, 1):
        for sign in (1, -1):
            part = 1 if sign == 1 else 2
            one = {
                "1": ((0, 0), (-sign, 0), 0, 0),
                "2": ((0, 0), (0, -sign), 1, 0),
                "3a": ((-sign, 0), (2, 0), 0, part),
                "3b": ((1, 0), (1, -sign), 1, 0),
                "4b": ((-1, 0), (-1, -sign), 1, 0),
                "5b": ((0, -sign), (0, 2), 1, part),
                "6": ((2, 0), (2, -sign), 1, 0),
                "7a": ((1, -sign), (1, 2), 1, part),
                "7b": ((-1, -sign), (-1, 2), 1, part),
                "8": ((2, -sign), (2, 2), 1, part),
            }[stage]
            found.append((lane, one[0], one[1], one[2], sign, one[3]))
    return found


def rows_of(part):
    return (0, HALF) if part == 0 else ((0, HALF // 2) if part == 1 else (HALF // 2, HALF // 2))


def kernel(
    act_ref, w_ref, g_ref, u_ref, len_hbm, wt_hbm, out_ref,
    u, w, gb, pf, cs, cr, sb, rr, rb, rabs, ra, ab, acc, len_ref, wt_ref,
    load_sem, xy_send, xy_recv, core_send, core_recv, rs_send, rs_recv,
    ag_send, ag_recv, fw_send, fw_recv, co_send, co_recv, az_send, az_recv, ac_send, ac_recv, out_sem,
):
    i, o = lax.axis_index("in"), lax.axis_index("out")
    z, c = lax.div(i, 2), lax.rem(i, 2)
    x, y = lax.div(o, 4), lax.rem(o, 4)
    width = ra.shape[1]
    half = rb.shape[2]

    def xy(axis, sign):
        if axis == 0:
            return (i, lax.rem(x + sign + 4, 4) * 4 + y)
        return (i, x * 4 + lax.rem(y + sign + 4, 4))

    def chip(d):
        return (lax.rem(z + d, 4) * 2 + c, o)

    other = (z * 2 + 1 - c, o)
    pending = []

    g_load = pltpu.make_async_copy(g_ref, gb.at[pl.ds(0, 2 * HALF)], load_sem.at[0])
    mine = pl.ds(pl.multiple_of(i * width, 128), width)
    a_load = pltpu.make_async_copy(act_ref, ab.at[:, mine], load_sem.at[1])
    u_load = pltpu.make_async_copy(u_ref, u, load_sem.at[2])
    w_load = pltpu.make_async_copy(w_ref, w, load_sem.at[3])
    len_load = pltpu.make_async_copy(len_hbm, len_ref, load_sem.at[4])
    wt_load = pltpu.make_async_copy(wt_hbm, wt_ref, load_sem.at[5])
    g_load.start()

    peers = [xy(0, 1), xy(0, -1), xy(1, 1), xy(1, -1), chip(1), chip(2), chip(3), other]
    barrier = pltpu.get_barrier_semaphore()
    for peer in peers:
        pl.semaphore_signal(barrier, inc=1, device_id=peer, device_id_type=MESH)
    for load in (a_load, u_load, w_load, len_load, wt_load):
        load.start()
    pl.semaphore_wait(barrier, len(peers))

    def remote(src, dst, send, recv, device):
        return pltpu.make_async_remote_copy(
            src_ref=src, dst_ref=dst, send_sem=send, recv_sem=recv, device_id=device, device_id_type=MESH
        )

    def token(lane, a, b):
        dx, dy = (b, a) if lane == 0 else (a, b)
        shard = lax.rem(x + dx + 4, 4) * 4 + lax.rem(y + dy + 4, 4)
        return shard * 2 * HALF + lane * HALF

    def xy_copy(kind, stage, at, arriving):
        lane, src, dst, axis, sign, part = moves(stage)[at]
        number = 4 * STAGES.index(stage) - 4 + at
        start, size = rows_of(part)
        if kind == 0:
            from_row, to_row, ref = OFFSET[(lane, *src)] + start, OFFSET[(lane, *dst)] + start, gb
        else:
            ref = ra
            from_row = pl.multiple_of(token(lane, *src) + start, 16)
            to_row = pl.multiple_of(token(lane, *dst) + start, 16) if arriving else from_row
        return remote(
            ref.at[pl.ds(from_row, size)], ref.at[pl.ds(to_row, size)],
            xy_send.at[kind, number], xy_recv.at[kind, number],
            xy(1 - axis if lane == 0 else axis, sign),
        )

    def issue(kind, *stages, start=True, record=True):
        for stage in stages:
            for at in range(4):
                copy = xy_copy(kind, stage, at, False)
                if start:
                    copy.start()
                if record:
                    pending.append(copy)

    def arrive(kind, *stages):
        for stage in stages:
            for at in range(4):
                xy_copy(kind, stage, at, True).wait_recv()

    def core_copy(q):
        row, m = GROUPS[q]
        return remote(cs.at[pl.ds(row, m)], cr.at[pl.ds(row, m)], core_send.at[q], core_recv.at[q], other)

    def s1(q, between=None):
        row, m = GROUPS[q]
        rows = pl.ds(row, m)

        def side(n, carry):
            cols = pl.ds(pl.multiple_of(lax.rem(1 - c + n, 2) * half, 128), half)
            pf[rows] = jnp.dot(gb[rows], u[:, cols], preferred_element_type=jnp.float32)

            @pl.when(n == 0)
            def _():
                cs[rows] = pf[rows].astype(cs.dtype)
                core_copy(q).start()
                if between is not None:
                    between()

            return carry

        lax.fori_loop(0, 2, side, 0)
        pending.append(core_copy(q))

    def rs_copy(q, d):
        row, m = GROUPS[q]
        n = m // 4
        there = lax.rem(z + d, 4)
        return remote(
            sb.at[pl.ds(pl.multiple_of(row + there * n, 16), n)], rr.at[d - 1, pl.ds(row // 4, n)],
            rs_send.at[q, d - 1], rs_recv.at[q, d - 1], chip(d),
        )

    def s2(q):
        row, m = GROUPS[q]
        core_copy(q).wait_recv()
        sb[pl.ds(row, m)] = (pf[pl.ds(row, m)] + cr[pl.ds(row, m)].astype(jnp.float32)).astype(sb.dtype)
        for d in (2, 1, 3):
            copy = rs_copy(q, d)
            copy.start()
            pending.append(copy)

    def piece(q, there):
        row, m = GROUPS[q]
        return pl.multiple_of(row + there * (m // 4), 16)

    def ag_copy(q, d, arriving):
        n = GROUPS[q][1] // 4
        at = piece(q, lax.rem(z - d + 4, 4) if arriving else z)
        block = rb.at[c, pl.ds(at, n)]
        return remote(block, block, ag_send.at[q, d - 1], ag_recv.at[q, d - 1], chip(d))

    def far(q):
        return q >= 5

    def s3(q):
        row, m = GROUPS[q]
        n = m // 4
        for d in (1, 2, 3):
            rs_copy(q, d).wait_recv()
        at = pl.ds(piece(q, z), n)
        total = pf[at] + cr[at].astype(jnp.float32)
        for d in (1, 2, 3):
            total = total + rr[d - 1, pl.ds(row // 4, n)].astype(jnp.float32)
        rb[c, at] = total.astype(rb.dtype)
        for d in (2, 1, 3) if far(q) else (1, 3):
            copy = ag_copy(q, d, False)
            copy.start()
            pending.append(copy)

    def fw_copy(q, way, arriving):
        n = GROUPS[q][1] // 4
        first = n // 32 * 16
        start, size = (0, first) if way == 0 else (first, n - first)
        at = piece(q, lax.rem(z + 2, 4) if arriving else lax.rem(z + (3 if way == 0 else 1), 4)) + start
        block = rb.at[c, pl.ds(pl.multiple_of(at, 16), size)]
        return remote(block, block, fw_send.at[q, way], fw_recv.at[q, way], chip(1 if way == 0 else 3))

    def s3b(q):
        if far(q):
            return
        for d, way in ((1, 0), (3, 1)):
            ag_copy(q, d, True).wait_recv()
            copy = fw_copy(q, way, False)
            copy.start()
            pending.append(copy)

    def co_copy(q, arriving):
        row, m = GROUPS[q]
        block = rb.at[1 - c if arriving else c, pl.ds(row, m)]
        return remote(block, block, co_send.at[q], co_recv.at[q], other)

    def s4(q):
        if far(q):
            for d in (1, 2, 3):
                ag_copy(q, d, True).wait_recv()
        else:
            for way in (0, 1):
                fw_copy(q, way, True).wait_recv()
        copy = co_copy(q, False)
        copy.start()
        pending.append(copy)

    def side_of(n):
        return c if n == 0 else 1 - c

    def s5(q, n):
        row, m = GROUPS[q]
        if n == 1:
            co_copy(q, True).wait_recv()
        h = side_of(n)
        for at in range(row // HALF, (row + m) // HALF):
            first = pl.multiple_of(token(*SLOTS[at]), 16)
            length = len_ref[lax.div(first, 4 * HALF)]
            position = lax.broadcasted_iota(jnp.int32, (HALF, half), 0) + lax.rem(first, 4 * HALF)
            block = rb[h, pl.ds(at * HALF, HALF)].astype(jnp.float32)
            rabs[h, pl.ds(first, HALF)] = jnp.where(position < length, block, 0.0).astype(rabs.dtype)

    def az_copy(d, arriving):
        from_z = lax.rem(z - d + 4, 4) if arriving else z
        block = ab.at[:, pl.ds(pl.multiple_of((from_z * 2 + c) * width, 128), width)]
        return remote(block, block, az_send.at[d - 1], az_recv.at[d - 1], chip(d))

    def ac_copy(d, arriving):
        there = lax.rem(z + d, 4) * 2 + (1 - c if arriving else c)
        block = ab.at[:, pl.ds(pl.multiple_of(there * width, 128), width)]
        return remote(block, block, ac_send.at[d], ac_recv.at[d], other)

    def rotate_act():
        for d in range(4):
            ac_copy(d, True).wait_recv()
        w_load.wait()
        first = pl.multiple_of(o * 2 * HALF, 16)
        for start in range(0, width, 256):
            size = min(256, width - start)
            ra[pl.ds(first, 2 * HALF), pl.ds(start, size)] = jnp.dot(
                ab[...], w[:, pl.ds(start, size)], preferred_element_type=jnp.float32
            ).astype(ra.dtype)

    h0 = lax.div(y, 2)
    sequences = [
        x * 2 + h0, x * 2 + 1 - h0,
        lax.rem(x + 1, 4) * 2 + h0, lax.rem(x + 3, 4) * 2 + h0,
        lax.rem(x + 1, 4) * 2 + 1 - h0, lax.rem(x + 3, 4) * 2 + 1 - h0,
        lax.rem(x + 2, 4) * 2 + h0, lax.rem(x + 2, 4) * 2 + 1 - h0,
    ]
    def weight_sum():
        total = wt_ref[0]
        for n in range(1, 8):
            total = total + wt_ref[n]
        return total.astype(jnp.float32)

    pieces = [(0, 0, half), (1, 0, 256), (1, 256, 256), (1, 512, half - 512)]

    def out_copy(number):
        n, start, size = pieces[number]
        rows = pl.ds(pl.multiple_of(side_of(n) * half + start, 8), size)
        return pltpu.make_async_copy(acc.at[rows], out_ref.at[rows], out_sem.at[number])

    def final(batch, n):
        last = batch[-1] == 7
        h = side_of(n)
        for number, (side, start, size) in enumerate(pieces if last else [(n, 0, half)]):
            if side != n:
                continue
            out = pl.ds(pl.multiple_of(h * half + start, 8), size)
            for s in batch:
                rows = pl.ds(pl.multiple_of(sequences[s] * 128, 128), 128)
                block = lax.dot_general(
                    rabs[h, rows, pl.ds(start, size)], ra[rows], (((0,), (0,)), ((), ())),
                    preferred_element_type=jnp.float32,
                )
                term = wt_ref[sequences[s]].astype(jnp.float32) * block * block
                total = term if s == 0 else acc[out] + term
                acc[out] = total / weight_sum() if s == 7 else total
            if last:
                out_copy(number).start()

    def first_act():
        a_load.wait()
        for d in (2, 1, 3):
            copy = az_copy(d, False)
            copy.start()
            pending.append(copy)

    def swap_act():
        for d in (0, 1, 2, 3):
            if d:
                az_copy(4 - d, True).wait_recv()
            copy = ac_copy(d, False)
            copy.start()
            pending.append(copy)

    g_load.wait()
    issue(0, "1", "2")
    first_act()
    u_load.wait()
    arrive(0, "1")
    issue(0, "3a", "3b", "4b")
    s1(0)
    swap_act()
    s2(0)
    arrive(0, "2")
    issue(0, "5b")
    s1(1)
    arrive(0, "3a")
    issue(0, "6")
    rotate_act()
    s2(1)
    s3(0)
    arrive(0, "3b")
    issue(0, "7a")
    s1(2)
    s2(2)
    s3(1)
    s3b(0)
    arrive(0, "4b")
    issue(0, "7b")
    arrive(0, "5b")
    s1(3)
    s2(3)
    s3(2)
    arrive(0, "6")
    issue(0, "8")
    issue(1, "1", "2")
    s1(4)
    s3b(1)
    len_load.wait()
    wt_load.wait()
    s4(0)
    s5(0, 0)
    s2(4)
    arrive(0, "7a", "7b")
    s1(5)
    s3(3)
    s2(5)
    arrive(0, "8")
    s1(6)
    s3b(2)
    s2(6)
    s4(1)
    arrive(1, "1")
    issue(1, "3a", "3b", "4b")
    s3(4)
    arrive(1, "2")
    issue(1, "5b")
    s5(1, 0)
    s5(0, 1)
    s3b(3)
    s5(1, 1)
    arrive(1, "3a")
    issue(1, "6")
    arrive(1, "3b")
    issue(1, "7a")
    s3(5)
    arrive(1, "4b")
    issue(1, "7b")
    s4(2)
    s5(2, 0)
    s3(6)
    s5(2, 1)
    s3b(4)
    s4(3)
    s5(3, 0)
    arrive(1, "5b")
    arrive(1, "6")
    issue(1, "8")
    final((0, 1, 2, 3), 0)
    s5(3, 1)
    final((0, 1, 2, 3), 1)
    s4(5)
    s5(5, 0)
    s4(4)
    s5(4, 0)
    s4(6)
    s5(6, 0)
    arrive(1, "7a", "7b")
    final((4, 5, 6), 0)
    arrive(1, "8")
    final((7,), 0)
    s5(5, 1)
    s5(4, 1)
    s5(6, 1)
    final((4, 5, 6), 1)
    final((7,), 1)

    for copy in pending:
        copy.wait_send()
    for number in range(len(pieces)):
        out_copy(number).wait()


def local(activations, act_basis, gradients, grad_basis, lengths, sample_weights):
    rows, wide = gradients.shape
    depth, cols = grad_basis.shape
    full, width = act_basis.shape
    tokens = 16 * rows
    groups = len(GROUPS)
    bf16, f32 = jnp.bfloat16, jnp.float32
    dma = pltpu.SemaphoreType.DMA
    anywhere = pl.BlockSpec(memory_space=pl.ANY)
    return pl.pallas_call(
        kernel,
        out_shape=jax.ShapeDtypeStruct((cols, width), f32),
        in_specs=[anywhere] * 6,
        out_specs=anywhere,
        scratch_shapes=[
            pltpu.VMEM((depth, cols), bf16),
            pltpu.VMEM((full, width), bf16),
            pltpu.VMEM((tokens, wide), bf16),
            pltpu.VMEM((tokens, cols // 2), f32),
            pltpu.VMEM((tokens, cols // 2), bf16),
            pltpu.VMEM((tokens, cols // 2), bf16),
            pltpu.VMEM((tokens, cols // 2), bf16),
            pltpu.VMEM((3, tokens // 4, cols // 2), bf16),
            pltpu.VMEM((2, tokens, cols // 2), bf16),
            pltpu.VMEM((2, tokens, cols // 2), bf16),
            pltpu.VMEM((tokens, width), bf16),
            pltpu.VMEM((rows, full), bf16),
            pltpu.VMEM((cols, width), f32),
            pltpu.SMEM((8,), jnp.int32),
            pltpu.SMEM((8,), jnp.int32),
            dma((6,)),
            dma((2, 40)), dma((2, 40)),
            dma((groups,)), dma((groups,)),
            dma((groups, 3)), dma((groups, 3)),
            dma((groups, 3)), dma((groups, 3)),
            dma((groups, 2)), dma((groups, 2)),
            dma((groups,)), dma((groups,)),
            dma((3,)), dma((3,)),
            dma((4,)), dma((4,)),
            dma((4,)),
        ],
        compiler_params=pltpu.CompilerParams(
            collective_id=0, has_side_effects=True, vmem_limit_bytes=56 * 1024 * 1024
        ),
    )(activations, act_basis, gradients, grad_basis, lengths, sample_weights)


def solution(mesh):
    in_specs = (P("out", "in"), P(None, "in"), P("out", "in"), P("in", "out"), P(), P())
    return jax.shard_map(local, mesh=mesh, in_specs=in_specs, out_specs=P("out", "in"), check_vma=False)
```
